512 devices in a mesh: cols: 4 (over y_lo), dom: 128 (over z, y_hi, x, core).
Axes of the slice: x: 4, y: 8 (y_hi: 2, y_lo: 4; y = y_hi * 4 + y_lo), z: 8, core: 2. Of those that a mesh axis runs over, the one named last changes fastest.
Arguments:
- features: bfloat16 [768, 65536], P('cols', 'dom'), may hold values from -6 to 6
- proj_in: bfloat16 [768, 256], P('cols'), may hold values from -0.3125 to 0.3125
- self_weight: bfloat16 [256, 256], replicated, may hold values from -0.375 to 0.375
- neigh_weight: bfloat16 [256, 256], replicated, may hold values from -0.375 to 0.375
- neighbors: int32 [16, 65536], P(None, 'dom'), may hold values from 0 to 8703, as said below
- degree: int32 [65536], P('dom'), may hold values from 1 to 16
- send_rows: int32 [128, 8192], P('dom'), may hold values from 0 to 511
- send_count: int32 [128, 128], P('dom'), may hold values from 0 to 64, as said below
Outputs:
- layer_out: bfloat16 [256, 65536], P('cols', 'dom')
The draws below stay inside these ranges and needn't reach their ends.
Inputs may be any that keep to these rules, and one draw needn't show every extreme that they name: `neighbors`: A code at or above 512 names a source partition other than the node's own and a slot below send_count of that source towards the node's partition. Every partition's rows are received in full (64 slots) from every other partition for at least one partition in every draw. `send_count`: zero on the diagonal; elsewhere 1 to 64, and 64 from every source towards at least one partition.
All inputs are finite; a program needn't handle non-finite values.
Results may differ from the reference program's by a relative error of at most 0.0051.
Values may be sent and summed in bfloat16 or wider, within the bound.
No kernel may reach another device: no remote copies, remote signals or barrier semaphores. Data moves between devices by JAX's collectives and lax.ppermute only.
A program may use at most 64 MiB of HBM per device.

```python
import jax
import jax.numpy as jnp
from jax import lax

D_IN = 768
HID = 256
NODE_DEV = 512
K = 16
CAP = 64
NODES = 65536
N_DOM = 128


def shared_counts(key):
    base = jax.random.fold_in(key, 7)
    key_hot, key_pick, key_low = jax.random.split(base, 3)
    hot = jax.random.randint(key_hot, (N_DOM,), 0, 4) == 0
    chosen = jax.random.randint(key_pick, (), 0, N_DOM)
    hot = jnp.logical_or(hot, jnp.arange(N_DOM) == chosen)
    low = jax.random.randint(key_low, (N_DOM, N_DOM), 1, CAP // 2 + 1)
    counts = jnp.where(hot[None, :], CAP, low)
    diagonal = jnp.arange(N_DOM)[:, None] == jnp.arange(N_DOM)[None, :]
    counts = jnp.where(diagonal, 0, counts).astype(jnp.int32)
    return (counts, hot)


def draw_send_count(key, part):
    return shared_counts(key)[0]


def draw_neighbors(key, part):
    counts, hot = shared_counts(key)
    inner = jax.random.fold_in(key, 11)
    key_local, key_roll, key_source, key_slot = jax.random.split(inner, 4)
    part_of = (jnp.arange(NODES) // NODE_DEV)[:, None]
    local = jax.random.randint(key_local, (NODES, K), 0, NODE_DEV)
    roll = jax.random.randint(key_roll, (NODES, K), 0, 8)
    remote = roll < jnp.where(hot[part_of], 4, 1)
    source = (part_of + 1 + jax.random.randint(key_source, (NODES, K), 0, N_DOM - 1)) % N_DOM
    limit = counts[source, part_of]
    slot = jax.random.randint(key_slot, (NODES, K), 0, 1 << 20) % limit
    code = jnp.where(remote, NODE_DEV + source * CAP + slot, local)
    return code.T.astype(jnp.int32)


def with_ends(result, rng, smallest, top_value):
    extent = result.shape
    place = [jax.random.randint(jax.random.fold_in(rng, axis), (), 0, extent[axis]) for axis in range(len(extent))]
    result = result.at[tuple(place)].set(smallest)
    longest = extent.index(max(extent))
    place[longest] = (place[longest] + 1) % extent[longest]
    return result.at[tuple(place)].set(top_value)


def strengthened(entries, stream_key, source, target, shards_of, factor):
    owner, partner = [(jnp.arange(entries.shape[axis_at]) // (entries.shape[axis_at] // shards_of)).reshape([-1 if axis == axis_at else 1 for axis in range(entries.ndim)]) for axis_at in (source, target)]
    chosen = jax.random.permutation(stream_key, shards_of)[partner]
    strong = (owner == chosen) | (owner == (partner + shards_of // 2) % shards_of)
    return jnp.where(strong, factor * entries, entries)


def level_of(stream_key, shape, shards, least, high):
    gain = 1.0
    for axis_at, blocks in shards:
        heights = jax.random.uniform(jax.random.fold_in(jax.random.fold_in(stream_key, 6), axis_at), (blocks,), jnp.float32, least / len(shards), high / len(shards))
        gain = gain * jnp.repeat(jnp.exp(heights), shape[axis_at] // blocks).reshape((-1,) + (1,) * (len(shape) - 1 - axis_at))
    return gain


def noise(own_key, dims, deviation, most, cuts=(), kind=jnp.bfloat16):
    drawn = deviation * jax.random.normal(own_key, dims, jnp.float32)
    if cuts:
        drawn = drawn * level_of(own_key, dims, cuts, -0.22, 0.18)
    return jnp.clip(drawn, -most, most).astype(kind)


def bell_draw_with(stream_key, dims, width, reach, cuts, heavy, held_as=jnp.bfloat16):
    array = width * jax.random.normal(stream_key, dims, jnp.float32)
    if cuts:
        array = array * level_of(stream_key, dims, cuts, -0.22, 0.18)
    return jnp.clip(strengthened(array, jax.random.fold_in(stream_key, 3), *heavy), -reach, reach).astype(held_as)


def setup_inputs(seed: int = 0) -> dict:
    streams_of = jax.random.split(jax.random.key(seed), 9)
    features = noise(streams_of[0], (D_IN, NODES), 1.0, 6.0, ((0, 4), (1, 128)))
    proj_in = bell_draw_with(streams_of[1], (D_IN, HID), D_IN ** -0.5, 0.3125, ((0, 4),), (0, 1, 4, 2.0))
    self_weight = noise(streams_of[2], (HID, HID), HID ** -0.5, 0.375)
    neigh_weight = noise(streams_of[3], (HID, HID), HID ** -0.5, 0.375)
    neighbors = draw_neighbors(jax.random.fold_in(streams_of[8], 71), 0)
    degree = with_ends(jax.random.randint(streams_of[5], (NODES,), 1, K + 1), jax.random.fold_in(streams_of[5], 1), 1, K).astype(jnp.int32)
    send_rows = with_ends(jax.random.randint(streams_of[6], (N_DOM, N_DOM * CAP), 0, NODE_DEV), jax.random.fold_in(streams_of[6], 1), 0, NODE_DEV - 1).astype(jnp.int32)
    send_count = draw_send_count(jax.random.fold_in(streams_of[8], 71), 0)
    return dict(features=features, proj_in=proj_in, self_weight=self_weight, neigh_weight=neigh_weight, neighbors=neighbors, degree=degree, send_rows=send_rows, send_count=send_count)


def reference(features, proj_in, self_weight, neigh_weight, neighbors, degree, send_rows, send_count):
    hidden = jnp.dot(features.T, proj_in, preferred_element_type=jnp.float32).astype(jnp.bfloat16)
    codes = neighbors.T.reshape(N_DOM, NODE_DEV, K)
    degs = degree.reshape(N_DOM, NODE_DEV)
    parts = jnp.arange(N_DOM, dtype=jnp.int32)

    def one_part(inputs):
        code, deg, part = inputs
        remote = code >= NODE_DEV
        rel = jnp.maximum(code - NODE_DEV, 0)
        source = rel // CAP
        slot = rel % CAP
        sent = send_rows[source, part * CAP + slot]
        valid = slot < send_count[source, part]
        rows = jnp.where(remote, source * NODE_DEV + sent, part * NODE_DEV + code).astype(jnp.int32)
        used = jnp.arange(K, dtype=jnp.int32)[None, :] < deg[:, None]
        keep = jnp.logical_and(used, jnp.logical_or(jnp.logical_not(remote), valid))
        picked = hidden[rows].astype(jnp.float32)
        total = jnp.sum(jnp.where(keep[:, :, None], picked, jnp.float32(0.0)), axis=1)
        return (total / deg[:, None].astype(jnp.float32)).astype(jnp.bfloat16)

    mean = lax.map(one_part, (codes, degs, parts)).reshape(NODES, HID)
    total = jnp.dot(hidden, self_weight, preferred_element_type=jnp.float32)
    total = total + jnp.dot(mean, neigh_weight, preferred_element_type=jnp.float32)
    return jnp.maximum(total, 0.0).astype(jnp.bfloat16).T
```

```python
import jax
import jax.numpy as jnp
from jax import lax
from jax.experimental import pallas as pl
from jax.experimental.pallas import tpu as pltpu
from jax.sharding import PartitionSpec as P

F32 = jnp.float32
BF16 = jnp.bfloat16
VMEM = pl.BlockSpec(memory_space=pltpu.VMEM)
LIMIT = pltpu.CompilerParams(vmem_limit_bytes=24 * 1024 * 1024)
CAP = 64
HALF = CAP // 2


def cost(flops, nbytes):
    return pl.CostEstimate(flops=flops, bytes_accessed=nbytes, transcendentals=0)


def dot(left, right, dims):
    return lax.dot_general(left, right, (dims, ((), ())), preferred_element_type=F32)


def partial_kernel(features, proj, weight, out):
    joined = dot(weight[...], proj[...], ((0,), (1,)))
    high = joined.astype(BF16)
    low = (joined - high.astype(F32)).astype(BF16)
    wide = dot(high, features[...], ((1,), (0,))) + dot(low, features[...], ((1,), (0,)))
    out[...] = wide.astype(out.dtype)


def partials(features, proj, weight, dtype):
    width, nodes = weight.shape[1], features.shape[1]
    return pl.pallas_call(
        partial_kernel,
        out_shape=jax.ShapeDtypeStruct((width, nodes), dtype),
        in_specs=[VMEM] * 3,
        out_specs=VMEM,
        compiler_params=LIMIT,
        cost_estimate=cost(2 * width * nodes * 640, 1 << 20),
    )(features, proj, weight)


def select_kernel(table, wanted, out):
    width, nodes = table.shape
    columns = wanted.shape[1]
    step = 256
    iota = lax.broadcasted_iota(jnp.int32, (256, step), 0).astype(F32).astype(BF16)
    for start in range(0, columns, step):
        halves = []
        for h in range(2):
            codes = wanted[pl.ds(h, 1), pl.ds(start, step)]
            total = jnp.zeros((width, step), F32)
            for base in range(0, nodes, 256):
                inside = jnp.logical_and(codes >= base, codes < base + 256)
                low = jnp.where(inside, codes - base, -1).astype(F32)
                low = jnp.broadcast_to(low, (16, step)).astype(BF16)
                low = jnp.broadcast_to(low[None], (16, 16, step)).reshape(256, step)
                onehot = jnp.where(iota == low, jnp.ones((), BF16), jnp.zeros((), BF16))
                total = total + dot(table[:, pl.ds(base, 256)], onehot, ((1,), (0,)))
            halves.append(total)
        out[pl.ds(start, step), :] = jnp.concatenate(halves, axis=0).T.astype(BF16)


def select(table, wanted):
    width, nodes = table.shape
    columns = wanted.shape[1]
    return pl.pallas_call(
        select_kernel,
        out_shape=jax.ShapeDtypeStruct((columns, 2 * width), BF16),
        in_specs=[VMEM] * 2,
        out_specs=VMEM,
        compiler_params=LIMIT,
        cost_estimate=cost(2 * width * nodes * 2 * columns, 1 << 20),
    )(table, wanted)


def count_kernel(codes, out, spread):
    slots, nodes = codes.shape
    rows = 64
    iota = lax.broadcasted_iota(jnp.int32, (rows // 16, 16, nodes), 0) * 16
    iota = iota + lax.broadcasted_iota(jnp.int32, (rows // 16, 16, nodes), 1)
    iota = iota.astype(F32).astype(BF16)
    one, zero = jnp.ones((), BF16), jnp.zeros((), BF16)

    def block(b, carry):
        low = codes[...] - b * 256
        low = jnp.where(jnp.logical_and(low >= 0, low < 256), low, -1).astype(F32)
        for k in range(slots):
            spread[k] = jnp.broadcast_to(low[k : k + 1], (16, nodes)).astype(BF16)
        for part in range(256 // rows):
            places = iota + jnp.asarray(part * rows, BF16)
            total = jnp.zeros((rows // 16, 16, nodes), BF16)
            for k in range(slots):
                total = total + jnp.where(places == spread[k][None], one, zero)
            out[pl.ds(b * 16 + part * (rows // 16), rows // 16)] = total
        return carry

    lax.fori_loop(0, out.shape[0] // 16, block, 0)


def count(codes, rows):
    slots, nodes = codes.shape
    counts = pl.pallas_call(
        count_kernel,
        out_shape=jax.ShapeDtypeStruct((rows // 16, 16, nodes), BF16),
        in_specs=[VMEM],
        out_specs=VMEM,
        scratch_shapes=[pltpu.VMEM((slots, 16, nodes), BF16)],
        compiler_params=LIMIT,
        cost_estimate=cost(2 * 10**10, 60 << 20),
    )(codes)
    return counts.reshape(rows, nodes)


def combine_kernel(table, rows, counts, own, degree, out):
    width, nodes = table.shape
    depth = rows.shape[0]
    turned = rows[...].astype(F32).T.astype(BF16)
    total = dot(table[...], counts[pl.ds(0, nodes), :], ((1,), (0,)))
    for h in range(2):
        part = counts[pl.ds(nodes + h * depth, depth), :]
        total = total + dot(turned[h * width : (h + 1) * width], part, ((1,), (0,)))
    result = own[...] + total / degree[...].astype(F32)
    out[...] = jnp.maximum(result, 0.0).astype(BF16)


def combine(table, rows, counts, own, degree):
    width, nodes = table.shape
    return pl.pallas_call(
        combine_kernel,
        out_shape=jax.ShapeDtypeStruct((width, nodes), BF16),
        in_specs=[VMEM] * 5,
        out_specs=VMEM,
        compiler_params=LIMIT,
        cost_estimate=cost(2 * width * nodes * 8704, 10 << 20),
    )(table, rows, counts, own, degree)


def local(features, proj_in, self_weight, neigh_weight, neighbors, degree, send_rows, send_count):
    slots, nodes = neighbors.shape

    sent = partials(features, proj_in, neigh_weight, BF16)
    width = sent.shape[0] // lax.axis_size("cols")
    sent = lax.all_to_all(sent.reshape(-1, width, nodes), "cols", 0, 0, tiled=True)

    live = jnp.arange(CAP, dtype=jnp.int32)[None, :] < send_count[0][:, None]
    wanted = jnp.where(live, send_rows[0].reshape(-1, CAP), -1)
    wanted = jnp.transpose(wanted.reshape(-1, 2, HALF), (1, 0, 2)).reshape(2, -1)

    used = jnp.arange(slots, dtype=jnp.int32)[:, None] < degree[None, :]
    code = neighbors - nodes
    part, slot = code >> 6, code & (CAP - 1)
    remote = nodes + (slot >> 5) * wanted.shape[1] + part * HALF + (slot & (HALF - 1))
    codes = jnp.where(used, jnp.where(code >= 0, remote, neighbors), -1)

    table = jnp.sum(sent.astype(F32), axis=0).astype(BF16)
    own = partials(features, proj_in, self_weight, F32)
    own = lax.psum_scatter(own, "cols", scatter_dimension=0, tiled=True)

    blocks = select(table, wanted).reshape(-1, HALF, 2 * width)
    rows = lax.all_to_all(blocks, "dom", 0, 0, tiled=True).reshape(-1, 2 * width)
    counts = count(codes, nodes + 2 * wanted.shape[1])
    return combine(table, rows, counts, own, degree[None, :])


def solution(mesh):
    return jax.shard_map(
        local,
        mesh=mesh,
        in_specs=(
            P("cols", "dom"),
            P("cols", None),
            P(),
            P(),
            P(None, "dom"),
            P("dom"),
            P("dom", None),
            P("dom", None),
        ),
        out_specs=P("cols", "dom"),
        check_vma=False,
    )
```

```python
import functools

import jax
import jax.numpy as jnp
from jax import lax
from jax.experimental import pallas as pl
from jax.experimental.pallas import tpu as pltpu
from jax.sharding import Mesh, PartitionSpec as P

F32 = jnp.float32
BF16 = jnp.bfloat16
VMEM = pl.BlockSpec(memory_space=pltpu.VMEM)
LIMIT = pltpu.CompilerParams(vmem_limit_bytes=24 * 1024 * 1024)
PLANE = ("z", "x", "core")
DOM = ("z", "yh", "x", "core")
CAP = 64
HALF = CAP // 2


def cost(flops, nbytes):
    return pl.CostEstimate(flops=flops, bytes_accessed=nbytes, transcendentals=0)


def dot(left, right, dims):
    return lax.dot_general(left, right, (dims, ((), ())), preferred_element_type=F32)


def partial_kernel(turn, features_hbm, proj_hbm, weight_hbm, out, features, proj, weight, wide, arrived):
    copies = [
        pltpu.make_async_copy(source, target, arrived.at[i])
        for i, (source, target) in enumerate(
            ((weight_hbm, weight), (proj_hbm, proj), (features_hbm, features))
        )
    ]
    for copy in copies:
        copy.start()
    copies[0].wait()
    copies[1].wait()
    joined = dot(weight[...], proj[...], ((0,), (1,)))
    high = joined.astype(BF16)
    low = (joined - high.astype(F32)).astype(BF16)
    copies[2].wait()
    total = dot(high, features[...], ((1,), (0,))) + dot(low, features[...], ((1,), (0,)))
    if not turn:
        out[...] = total.astype(out.dtype)
        return
    wide[...] = total
    blocks = lax.axis_size("cols")
    depth = total.shape[0] // blocks
    me = lax.axis_index("cols")
    for s in range(blocks):
        start = pl.multiple_of(lax.rem(me + s, blocks) * depth, depth)
        out[pl.ds(s * depth, depth), :] = wide[pl.ds(start, depth), :].astype(out.dtype)


def partials(features, proj, weight, dtype, turn):
    width, nodes = weight.shape[1], features.shape[1]
    return pl.pallas_call(
        functools.partial(partial_kernel, turn),
        out_shape=jax.ShapeDtypeStruct((width, nodes), dtype),
        in_specs=[pl.BlockSpec(memory_space=pl.ANY)] * 3,
        out_specs=VMEM,
        scratch_shapes=[
            pltpu.VMEM(features.shape, BF16),
            pltpu.VMEM(proj.shape, BF16),
            pltpu.VMEM(weight.shape, BF16),
            pltpu.VMEM((width, nodes), F32),
            pltpu.SemaphoreType.DMA((3,)),
        ],
        compiler_params=LIMIT,
        cost_estimate=cost(2 * width * nodes * 640, 1 << 20),
    )(*(pltpu.with_memory_space_constraint(array, pltpu.HBM) for array in (features, proj, weight)))


def select_kernel(near, far, wanted, out):
    width, nodes = near.shape
    tables = (near, far)
    columns = wanted.shape[2]
    step = 256
    places = step // HALF
    iota = lax.broadcasted_iota(jnp.int32, (256, step), 0).astype(F32).astype(BF16)
    for start in range(0, columns, step):
        for t in range(2):
            halves = []
            for h in range(2):
                codes = wanted[t, pl.ds(h, 1), pl.ds(start, step)]
                total = jnp.zeros((width, step), F32)
                for base in range(0, nodes, 256):
                    inside = jnp.logical_and(codes >= base, codes < base + 256)
                    low = jnp.where(inside, codes - base, -1).astype(F32)
                    low = jnp.broadcast_to(low, (16, step)).astype(BF16)
                    low = jnp.broadcast_to(low[None], (16, 16, step)).reshape(256, step)
                    onehot = jnp.where(iota == low, jnp.ones((), BF16), jnp.zeros((), BF16))
                    total = total + dot(tables[t][:, pl.ds(base, 256)], onehot, ((1,), (0,)))
                halves.append(total)
            rows = jnp.concatenate(halves, axis=0).T.astype(BF16).reshape(places, HALF, 2 * width)
            out[pl.ds(start // HALF, places), pl.ds(t * HALF, HALF), :] = rows


def select(near, far, wanted):
    width, nodes = near.shape
    columns = wanted.shape[2]
    return pl.pallas_call(
        select_kernel,
        out_shape=jax.ShapeDtypeStruct((columns // HALF, CAP, 2 * width), BF16),
        in_specs=[VMEM] * 3,
        out_specs=VMEM,
        compiler_params=LIMIT,
        cost_estimate=cost(8 * width * nodes * columns, 1 << 20),
    )(near, far, wanted)


def count_kernel(first, codes, out, spread, stage, left):
    slots, nodes = codes.shape
    rows = 64
    blocks = out.shape[0] // 16
    iota = lax.broadcasted_iota(jnp.int32, (rows // 16, 16, nodes), 0) * 16
    iota = iota + lax.broadcasted_iota(jnp.int32, (rows // 16, 16, nodes), 1)
    iota = iota.astype(F32).astype(BF16)
    one, zero = jnp.ones((), BF16), jnp.zeros((), BF16)

    def move(b, turn):
        return pltpu.make_async_copy(stage.at[turn], out.at[pl.ds(b * 16, 16)], left.at[turn])

    def block(b, carry):
        turn = lax.rem(b, 2)

        @pl.when(b >= 2)
        def _():
            move(b - 2, turn).wait()

        low = codes[...] - (first + b) * 256
        low = jnp.where(jnp.logical_and(low >= 0, low < 256), low, -1).astype(F32)
        for k in range(slots):
            spread[k] = jnp.broadcast_to(low[k : k + 1], (16, nodes)).astype(BF16)
        for part in range(256 // rows):
            places = iota + jnp.asarray(part * rows, BF16)
            total = jnp.zeros((rows // 16, 16, nodes), BF16)
            for k in range(slots):
                total = total + jnp.where(places == spread[k][None], one, zero)
            stage[turn, pl.ds(part * (rows // 16), rows // 16)] = total
        move(b, turn).start()
        return carry

    lax.fori_loop(0, blocks, block, 0)
    for b in range(blocks - 2, blocks):
        move(b, b % 2).wait()


def count(codes, first, blocks):
    slots, nodes = codes.shape
    counts = pl.pallas_call(
        functools.partial(count_kernel, first),
        out_shape=pltpu.HBM((blocks * 16, 16, nodes), BF16),
        in_specs=[VMEM],
        out_specs=pl.BlockSpec(memory_space=pl.ANY),
        scratch_shapes=[
            pltpu.VMEM((slots, 16, nodes), BF16),
            pltpu.VMEM((2, 16, 16, nodes), BF16),
            pltpu.SemaphoreType.DMA((2,)),
        ],
        compiler_params=LIMIT,
        cost_estimate=cost(blocks * 5 * 10**8, blocks << 20),
    )(codes)
    return counts.reshape(blocks * 256, nodes)


def combine_kernel(splits, table, rows, degree, *refs):
    counts_hbm, refs = refs[: len(splits)], refs[len(splits) :]
    parts, (out, counts, arrived) = refs[:-3], refs[-3:]
    width, nodes = table.shape
    depth = rows.shape[0]
    chunk = 512
    copies = []
    for source, extent in zip(counts_hbm, splits):
        for low in range(0, extent, chunk):
            target = counts.at[pl.ds(len(copies) * chunk, chunk)]
            copy = pltpu.make_async_copy(source.at[pl.ds(low, chunk)], target, arrived.at[len(copies)])
            copy.start()
            copies.append(copy)
    turned = rows[...].astype(F32).T.astype(BF16)
    total = jnp.zeros((width, nodes), F32)
    for i, copy in enumerate(copies):
        start = i * chunk
        if start < nodes:
            left = table[:, start : start + chunk]
        else:
            h, low = divmod(start - nodes, depth)
            left = turned[h * width : (h + 1) * width, low : low + chunk]
        copy.wait()
        total = total + dot(left, counts[pl.ds(start, chunk), :], ((1,), (0,)))
    result = total / degree[...].astype(F32)
    for part in parts:
        result = result + part[...]
    out[...] = jnp.maximum(result, 0.0).astype(BF16)


def combine(table, rows, degree, counts, parts):
    width, nodes = table.shape
    splits = [part.shape[0] for part in counts]
    hbm = [pltpu.with_memory_space_constraint(part, pltpu.HBM) for part in counts]
    return pl.pallas_call(
        functools.partial(combine_kernel, splits),
        out_shape=jax.ShapeDtypeStruct((width, nodes), BF16),
        in_specs=[VMEM] * 3 + [pl.BlockSpec(memory_space=pl.ANY)] * len(hbm) + [VMEM] * len(parts),
        out_specs=VMEM,
        scratch_shapes=[
            pltpu.VMEM((sum(splits), nodes), BF16),
            pltpu.SemaphoreType.DMA((sum(splits) // 512,)),
        ],
        compiler_params=LIMIT,
        cost_estimate=cost(2 * width * nodes * 8704, 10 << 20),
    )(table, rows, degree, *hbm, *parts)


def local(features, proj_in, self_weight, neigh_weight, neighbors, degree, send_rows, send_count):
    slots, nodes = neighbors.shape
    columns = lax.axis_size("cols")
    mine = lax.axis_index("yh")
    swap = [(0, 1), (1, 0)]

    sent = partials(features, proj_in, neigh_weight, BF16, False)
    sent, send_rows, send_count, neighbors = lax.optimization_barrier((sent, send_rows, send_count, neighbors))

    live = jnp.arange(CAP, dtype=jnp.int32)[None, :] < send_count[0][:, None]
    wanted = jnp.where(live, send_rows[0].reshape(-1, CAP), -1)
    wanted = wanted.reshape(lax.axis_size("z"), 2, -1, 2, HALF)
    wanted = jnp.transpose(wanted, (1, 3, 0, 2, 4)).reshape(2, 2, -1)
    here = jnp.where(mine == 0, wanted[0], wanted[1])
    there = jnp.where(mine == 0, wanted[1], wanted[0])
    wanted = jnp.stack([here, lax.ppermute(there, "yh", swap)])
    depth = 2 * wanted.shape[2]

    used = jnp.arange(slots, dtype=jnp.int32)[:, None] < degree[None, :]
    code = neighbors - nodes
    part, slot = code >> 6, code & (CAP - 1)
    place = (part >> 4) * 8 + (part & 7)
    far = ((part >> 3) & 1) ^ mine
    remote = nodes + (slot >> 5) * depth + place * CAP + far * HALF + (slot & (HALF - 1))
    codes = jnp.where(used, jnp.where(code >= 0, remote, neighbors), -1)

    width = sent.shape[0] // columns
    sent = lax.all_to_all(sent.reshape(-1, width, nodes), "cols", 0, 0, tiled=True)
    own = partials(features, proj_in, self_weight, F32, True)

    table = jnp.sum(sent.astype(F32), axis=0).astype(BF16)
    codes, table = lax.optimization_barrier((codes, table))
    partner = lax.ppermute(table, "yh", swap)
    blocks = (nodes + 2 * depth) // 256
    early = blocks // 4 // 2 * 2
    counts = [count(codes, 0, early)]
    wanted, counts[0] = lax.optimization_barrier((wanted, counts[0]))
    chosen = select(table, partner, wanted)
    chosen, own = lax.optimization_barrier((chosen, own))
    rows = lax.all_to_all(chosen, PLANE, 0, 0, tiled=True).reshape(-1, 2 * width)

    parts = [own[:width]]
    for s in range(1, columns):
        ring = [(c, (c + s) % columns) for c in range(columns)]
        parts.append(lax.ppermute(own[s * width : (s + 1) * width], "cols", ring))
    counts.append(count(codes, early, blocks - early))
    return combine(table, rows, degree[None, :], counts, parts)


def solution(mesh):
    fine = Mesh(mesh.devices.reshape(4, 8, 2, 4, 2), ("cols",) + DOM)
    return jax.shard_map(
        local,
        mesh=fine,
        in_specs=(
            P("cols", DOM),
            P("cols", None),
            P(),
            P(),
            P(None, DOM),
            P(DOM),
            P(DOM, None),
            P(DOM, None),
        ),
        out_specs=P("cols", DOM),
        check_vma=False,
    )
```

```python
import functools

import jax
import jax.numpy as jnp
from jax import lax
from jax.experimental import pallas as pl
from jax.experimental.pallas import tpu as pltpu
from jax.sharding import PartitionSpec as P

F32 = jnp.float32
BF16 = jnp.bfloat16
F8 = jnp.float8_e4m3fn
VMEM = pl.BlockSpec(memory_space=pltpu.VMEM)
LIMIT = pltpu.CompilerParams(vmem_limit_bytes=24 * 1024 * 1024)
CAP = 64
PACK, BITS = 6, 5
HALF = CAP // 2


def cost(flops, nbytes):
    return pl.CostEstimate(flops=flops, bytes_accessed=nbytes, transcendentals=0)


def dot(left, right, dims):
    return lax.dot_general(left, right, (dims, ((), ())), preferred_element_type=F32)


def partial_kernel(turn, features_hbm, proj_hbm, weight_hbm, out, features, proj, weight, wide, arrived):
    pairs = ((proj_hbm, proj), (weight_hbm, weight), (features_hbm, features))
    copies = [pltpu.make_async_copy(*pair, arrived.at[i]) for i, pair in enumerate(pairs)]
    for copy in copies:
        copy.start()
    copies[0].wait()
    copies[1].wait()
    joined = dot(weight[...], proj[...], ((0,), (1,)))
    high = joined.astype(BF16)
    low = (joined - high.astype(F32)).astype(BF16)
    copies[2].wait()
    total = dot(high, features[...], ((1,), (0,))) + dot(low, features[...], ((1,), (0,)))
    columns, depth = out.shape[0], out.shape[1]
    if not turn:
        out[...] = total.astype(BF16).reshape(out.shape)
        return
    wide[...] = total
    me = lax.axis_index("cols")
    for s in range(columns):
        start = pl.multiple_of(lax.rem(me + s, columns) * depth, depth)
        out[s] = wide[pl.ds(start, depth), :].astype(BF16)


def partials(features, proj, weight, columns, turn):
    width, nodes = weight.shape[1], features.shape[1]
    arrays = (features, proj, weight)
    return pl.pallas_call(
        functools.partial(partial_kernel, turn),
        out_shape=jax.ShapeDtypeStruct((columns, width // columns, nodes), BF16),
        in_specs=[pl.BlockSpec(memory_space=pl.ANY)] * 3,
        out_specs=VMEM,
        scratch_shapes=[pltpu.VMEM(array.shape, BF16) for array in arrays]
        + [pltpu.VMEM((width, nodes), F32), pltpu.SemaphoreType.DMA((3,))],
        compiler_params=LIMIT,
        cost_estimate=cost(2 * width * nodes * 640, 1 << 20),
    )(*(pltpu.with_memory_space_constraint(array, pltpu.HBM) for array in arrays))


def select_kernel(sent, wanted, rows, table):
    width, nodes = table.shape
    total = sent[0].astype(F32)
    for c in range(1, sent.shape[0]):
        total = total + sent[c].astype(F32)
    table[...] = total.astype(BF16)
    step = 256
    iota = lax.broadcasted_iota(jnp.int32, (256, step), 0).astype(F32).astype(BF16)
    for start in range(0, wanted.shape[1], step):
        halves = []
        for h in range(2):
            codes = wanted[pl.ds(h, 1), pl.ds(start, step)]
            picked = jnp.zeros((width, step), F32)
            for base in range(0, nodes, 256):
                inside = jnp.logical_and(codes >= base, codes < base + 256)
                low = jnp.where(inside, codes - base, -1).astype(F32)
                low = jnp.broadcast_to(low, (16, step)).astype(BF16)
                low = jnp.broadcast_to(low[None], (16, 16, step)).reshape(256, step)
                onehot = jnp.where(iota == low, jnp.ones((), BF16), jnp.zeros((), BF16))
                picked = picked + dot(table[:, pl.ds(base, 256)], onehot, ((1,), (0,)))
            halves.append(picked)
        rows[pl.ds(start, step), :] = jnp.concatenate(halves, axis=0).T.astype(BF16)


def select(sent, wanted):
    width, nodes = sent.shape[1], sent.shape[2]
    columns = wanted.shape[1]
    return pl.pallas_call(
        select_kernel,
        out_shape=(
            jax.ShapeDtypeStruct((columns, 2 * width), BF16),
            jax.ShapeDtypeStruct((width, nodes), BF16),
        ),
        in_specs=[VMEM] * 2,
        out_specs=(VMEM,) * 2,
        compiler_params=LIMIT,
        cost_estimate=cost(4 * width * nodes * columns, 1 << 20),
    )(sent, wanted)


def count_kernel(codes, out, spread, stage, left):
    slots, nodes = codes.shape
    block, strip = stage.shape[1] // PACK, 32
    span = PACK * block
    iota = lax.broadcasted_iota(jnp.int32, (strip, nodes), 0)

    def move(i, size, turn):
        return pltpu.make_async_copy(
            stage.at[turn, pl.ds(0, size)], out.at[pl.ds(i * span, size)], left.at[turn]
        )

    def group(i, turn):
        code = codes[...] - i * span
        inside = jnp.logical_and(code >= 0, code < span)
        spread[0] = jnp.where(inside, code & (block - 1), -1)
        spread[1] = jnp.where(inside, 1 << ((code >> 7) * BITS), 0)
        for low in range(0, block, strip):
            places = iota + low
            total = jnp.zeros((strip, nodes), jnp.int32)
            for k in range(slots):
                total = total + jnp.where(places == spread[0, k : k + 1, :], spread[1, k : k + 1, :], 0)
            for j in range(PACK):
                part = (total >> (j * BITS)) & (2**BITS - 1)
                stage[turn, pl.ds(j * block + low, strip), :] = part.astype(F32).astype(out.dtype)

    def step(i, carry):
        turn = lax.rem(i, 2)

        @pl.when(i >= 2)
        def _():
            move(i - 2, span, turn).wait()

        group(i, turn)
        move(i, span, turn).start()
        return carry

    last = pl.cdiv(out.shape[0], span) - 1
    lax.fori_loop(0, last, step, 0)
    move(last - 2, span, last % 2).wait()
    group(last, last % 2)
    move(last, out.shape[0] - last * span, last % 2).start()
    move(last - 1, span, (last - 1) % 2).wait()
    move(last, out.shape[0] - last * span, last % 2).wait()


def count(codes, rows):
    slots, nodes = codes.shape
    return pl.pallas_call(
        count_kernel,
        out_shape=pltpu.HBM((rows, nodes), F8),
        in_specs=[VMEM],
        out_specs=pl.BlockSpec(memory_space=pl.ANY),
        scratch_shapes=[
            pltpu.VMEM((2, slots, nodes), jnp.int32),
            pltpu.VMEM((2, PACK * 128, nodes), F8),
            pltpu.SemaphoreType.DMA((2,)),
        ],
        compiler_params=LIMIT,
        cost_estimate=cost(9 * 10**9, 20 << 20),
    )(codes)


def combine_kernel(table, rows, degree, counts_hbm, *refs):
    parts, (out, counts, arrived) = refs[:-3], refs[-3:]
    width, nodes = table.shape
    depth = rows.shape[0]
    chunk = 512
    copies = []
    for i in range(counts.shape[0] // chunk):
        at = pl.ds(i * chunk, chunk)
        copies.append(pltpu.make_async_copy(counts_hbm.at[at], counts.at[at], arrived.at[i]))
        copies[i].start()
    turned = rows[...].astype(F32).T.astype(BF16)
    total = jnp.zeros((width, nodes), F32)
    for i, copy in enumerate(copies):
        start = i * chunk
        if start < nodes:
            left = table[:, start : start + chunk]
        else:
            h, low = divmod(start - nodes, depth)
            left = turned[h * width : (h + 1) * width, low : low + chunk]
        copy.wait()
        total = total + dot(left, counts[pl.ds(start, chunk), :].astype(BF16), ((1,), (0,)))
    result = total / degree[...].astype(F32)
    for part in parts:
        result = result + part[...].astype(F32)
    out[...] = jnp.maximum(result, 0.0).astype(BF16)


def combine(table, rows, degree, counts, parts):
    width, nodes = table.shape
    return pl.pallas_call(
        combine_kernel,
        out_shape=jax.ShapeDtypeStruct((width, nodes), BF16),
        in_specs=[VMEM] * 3 + [pl.BlockSpec(memory_space=pl.ANY)] + [VMEM] * len(parts),
        out_specs=VMEM,
        scratch_shapes=[pltpu.VMEM(counts.shape, F8), pltpu.SemaphoreType.DMA((counts.shape[0] // 512,))],
        compiler_params=LIMIT,
        cost_estimate=cost(2 * width * nodes * 8704, 10 << 20),
    )(table, rows, degree, pltpu.with_memory_space_constraint(counts, pltpu.HBM), *parts)


def local(features, proj_in, self_weight, neigh_weight, neighbors, degree, send_rows, send_count):
    slots, nodes = neighbors.shape
    columns = lax.axis_size("cols")
    sent = partials(features, proj_in, neigh_weight, columns, False)
    sent, send_rows, send_count, neighbors = lax.optimization_barrier((sent, send_rows, send_count, neighbors))
    sent = lax.all_to_all(sent, "cols", 0, 0, tiled=True)

    live = jnp.arange(CAP, dtype=jnp.int32).reshape(1, 2, HALF) < send_count.reshape(-1, 1, 1)
    wanted = jnp.where(live, send_rows.reshape(-1, 2, HALF), -1)
    wanted = jnp.transpose(wanted, (1, 0, 2)).reshape(2, -1)
    depth = wanted.shape[1]

    used = jnp.arange(slots, dtype=jnp.int32)[:, None] < degree[None, :]
    code = neighbors - nodes
    part, slot = code >> 6, code & (CAP - 1)
    remote = nodes + (slot >> 5) * depth + part * HALF + (slot & (HALF - 1))
    codes = jnp.where(used, jnp.where(code >= 0, remote, neighbors), -1)

    own = partials(features, proj_in, self_weight, columns, True)
    chosen, table = select(sent, wanted)
    chosen, codes, own = lax.optimization_barrier((chosen, codes, own))
    rows = lax.all_to_all(chosen.reshape(-1, HALF, chosen.shape[1]), "dom", 0, 0, tiled=True)
    parts = [own[0]]
    for s in range(1, columns):
        parts.append(lax.ppermute(own[s], "cols", [(c, (c + s) % columns) for c in range(columns)]))
    counts = count(codes, nodes + 2 * depth)
    return combine(table, rows.reshape(chosen.shape), degree[None, :], counts, parts)


def solution(mesh):
    return jax.shard_map(
        local,
        mesh=mesh,
        in_specs=(
            P("cols", "dom"),
            P("cols", None),
            P(),
            P(),
            P(None, "dom"),
            P("dom"),
            P("dom", None),
            P("dom", None),
        ),
        out_specs=P("cols", "dom"),
        check_vma=False,
    )
```

```python
import jax
import jax.numpy as jnp
from jax import lax
from jax.experimental import pallas as pl
from jax.experimental.pallas import tpu as pltpu
from jax.sharding import PartitionSpec as P

F32 = jnp.float32
BF16 = jnp.bfloat16
F8 = jnp.float8_e4m3fn
VMEM = pl.BlockSpec(memory_space=pltpu.VMEM)
ANY = pl.BlockSpec(memory_space=pl.ANY)
LIMIT = pltpu.CompilerParams(vmem_limit_bytes=24 * 1024 * 1024)
CAP = 64
PACK, BITS = 6, 5
HALF = CAP // 2


def cost(flops, nbytes):
    return pl.CostEstimate(flops=flops, bytes_accessed=nbytes, transcendentals=0)


def dot(left, right, dims):
    return lax.dot_general(left, right, (dims, ((), ())), preferred_element_type=F32)


def fetch(sources, targets, arrived):
    copies = [pltpu.make_async_copy(*pair, arrived.at[i]) for i, pair in enumerate(zip(sources, targets))]
    for copy in copies:
        copy.start()
    return copies


def product(copies, weight, proj, features):
    copies[0].wait()
    copies[1].wait()
    joined = dot(weight[...], proj[...], ((0,), (1,)))
    high = joined.astype(BF16)
    low = (joined - high.astype(F32)).astype(BF16)
    copies[2].wait()
    return dot(high, features[...], ((1,), (0,))) + dot(low, features[...], ((1,), (0,)))


def scratch_of(arrays):
    return [pltpu.VMEM(array.shape, array.dtype) for array in arrays] + [pltpu.SemaphoreType.DMA((len(arrays),))]


def in_hbm(arrays):
    return [pltpu.with_memory_space_constraint(array, pltpu.HBM) for array in arrays]


def sent_kernel(weight_hbm, proj_hbm, features_hbm, out, weight, proj, features, arrived):
    copies = fetch((weight_hbm, proj_hbm, features_hbm), (weight, proj, features), arrived)
    out[...] = product(copies, weight, proj, features).astype(BF16).reshape(out.shape)


def sent_partials(weight, proj, features, columns):
    width, nodes = weight.shape[1], features.shape[1]
    arrays = (weight, proj, features)
    return pl.pallas_call(
        sent_kernel,
        out_shape=jax.ShapeDtypeStruct((columns, width // columns, nodes), BF16),
        in_specs=[ANY] * 3,
        out_specs=VMEM,
        scratch_shapes=scratch_of(arrays),
        compiler_params=LIMIT,
        cost_estimate=cost(2 * width * nodes * 640, 1 << 20),
    )(*in_hbm(arrays))


def side_kernel(*refs):
    sources, (kept, given, wanted), targets = refs[:5], refs[5:8], refs[8:13]
    arrived, wide, spread, limits = refs[13:]
    weight, proj, features, rows, live = targets
    copies = fetch(sources, targets, arrived)
    wide[...] = product(copies, weight, proj, features)
    depth = kept.shape[1]
    me = lax.axis_index("cols")
    pair, odd = me // 2, lax.rem(me, 2)
    for i in range(2):
        first = 2 * (pair if i == 0 else 1 - pair)
        start = pl.multiple_of((first + odd) * depth, depth)
        kept[i] = wide[pl.ds(start, depth), :]
        start = pl.multiple_of((first + 1 - odd) * depth, depth)
        given[i] = wide[pl.ds(start, depth), :].astype(BF16)
    copies[3].wait()
    copies[4].wait()
    lines = spread.shape[0]
    for i in range(lines):
        spread[pl.ds(i, 1), :] = rows[:, pl.ds(i * 128, 128)]
    limits[...] = jnp.broadcast_to(live[...], limits.shape).astype(F32).T
    lane = lax.broadcasted_iota(jnp.int32, (lines // 2, 128), 1)
    halves = []
    for k in range(2):
        low = limits[pl.ds(2 * k, lines // 2, stride=4), :]
        high = limits[pl.ds(2 * k + 1, lines // 2, stride=4), :]
        alive = (lane & (CAP - 1)).astype(F32) < jnp.where(lane < CAP, low, high)
        halves.append(jnp.where(alive, spread[pl.ds(k, lines // 2, stride=2), :], -1))
    even, odd = halves
    for h in range(2):
        parts = [pltpu.roll(source, (128 + to - HALF * h) % 128, 1) for source, to in ((even, 0), (even, -32), (odd, 64), (odd, 32))]
        wanted[h] = jnp.where(
            lane < 64, jnp.where(lane < 32, parts[0], parts[1]), jnp.where(lane < 96, parts[2], parts[3])
        )


def side(weight, proj, features, send_rows, send_count, columns):
    width, nodes = weight.shape[1], features.shape[1]
    depth = width // columns
    lines = send_rows.shape[1] // 128
    arrays = (weight, proj, features, send_rows, send_count)
    return pl.pallas_call(
        side_kernel,
        out_shape=(
            jax.ShapeDtypeStruct((2, depth, nodes), F32),
            jax.ShapeDtypeStruct((2, depth, nodes), BF16),
            jax.ShapeDtypeStruct((2, lines // 2, 128), jnp.int32),
        ),
        in_specs=[ANY] * 5,
        out_specs=(VMEM,) * 3,
        scratch_shapes=scratch_of(arrays)
        + [
            pltpu.VMEM((width, nodes), F32),
            pltpu.VMEM((lines, 128), jnp.int32),
            pltpu.VMEM((send_count.shape[1], 128), F32),
        ],
        compiler_params=LIMIT,
        cost_estimate=cost(2 * width * nodes * 640, 1 << 20),
    )(*in_hbm(arrays))


def select_kernel(sent, wanted, rows_hbm, table, rows, left):
    width, nodes = table.shape
    total = sent[0].astype(F32)
    for c in range(1, sent.shape[0]):
        total = total + sent[c].astype(F32)
    table[...] = total.astype(BF16)
    stacked = jnp.concatenate([table[:, :256], table[:, 256:]], axis=0)
    step = 256
    iota = lax.broadcasted_iota(jnp.int32, (256, step), 0).astype(F32).astype(BF16)
    copies = []
    for start in range(0, rows.shape[0], step):
        halves = []
        for h in range(2):
            lines = [wanted[h, pl.ds((start + at) // 128, 1), :] for at in range(0, step, 128)]
            codes = jnp.concatenate(lines, axis=1)
            low = jnp.where(codes >= 0, codes & 255, -1).astype(F32)
            low = jnp.broadcast_to(low, (16, step)).astype(BF16)
            low = jnp.broadcast_to(low[None], (16, 16, step)).reshape(256, step)
            onehot = jnp.where(iota == low, jnp.ones((), BF16), jnp.zeros((), BF16))
            both = dot(stacked, onehot, ((1,), (0,)))
            picked = jnp.where(codes >= 256, both[width:], both[:width])
            halves.append(picked)
        at = pl.ds(start, step)
        rows[at, :] = jnp.concatenate(halves, axis=0).T.astype(BF16)
        copies.append(pltpu.make_async_copy(rows.at[at], rows_hbm.at[at], left.at[len(copies)]))
        copies[-1].start()
    for copy in copies:
        copy.wait()


def select(sent, wanted):
    width, nodes = sent.shape[1], sent.shape[2]
    columns = wanted.shape[1] * 128
    return pl.pallas_call(
        select_kernel,
        out_shape=(
            pltpu.HBM((columns, 2 * width), BF16),
            jax.ShapeDtypeStruct((width, nodes), BF16),
        ),
        in_specs=[VMEM] * 2,
        out_specs=(ANY, VMEM),
        scratch_shapes=[pltpu.VMEM((columns, 2 * width), BF16), pltpu.SemaphoreType.DMA((columns // 256,))],
        compiler_params=LIMIT,
        cost_estimate=cost(4 * width * nodes * columns, 1 << 20),
    )(sent, wanted)


def count_kernel(neighbors_hbm, degree_hbm, near, far, neighbors, degree, arrived, codes, spread, stage, left):
    slots, nodes = codes.shape
    for copy in fetch((neighbors_hbm, degree_hbm), (neighbors, degree), arrived):
        copy.wait()
    rows = near.shape[0] + far.shape[0]
    code = neighbors[...] - nodes
    part, slot = code >> 6, code & (CAP - 1)
    remote = nodes + (slot >> 5) * ((rows - nodes) // 2) + part * HALF + (slot & (HALF - 1))
    used = lax.broadcasted_iota(jnp.int32, (slots, nodes), 0) < degree[...]
    codes[...] = jnp.where(used, jnp.where(code >= 0, remote, code + nodes), -1)
    block, strip = stage.shape[1] // PACK, 32
    span = PACK * block
    iota = lax.broadcasted_iota(jnp.int32, (strip, nodes), 0)

    def group(i, write):
        code = codes[...] - i * span
        inside = jnp.logical_and(code >= 0, code < span)
        spread[0] = jnp.where(inside, code & (block - 1), -1)
        spread[1] = jnp.where(inside, 1 << ((code >> 7) * BITS), 0)
        for low in range(0, block, strip):
            places = iota + low
            total = jnp.zeros((strip, nodes), jnp.int32)
            for k in range(slots):
                total = total + jnp.where(places == spread[0, k : k + 1, :], spread[1, k : k + 1, :], 0)
            for j in range(PACK):
                part = (total >> (j * BITS)) & (2**BITS - 1)
                write(j * block + low, part.astype(F32).astype(F8))

    def near_step(i, carry):
        def write(low, part):
            near[pl.ds(pl.multiple_of(i * span + low, strip), strip), :] = part

        group(i, write)
        return carry

    def move(i, size, turn):
        return pltpu.make_async_copy(
            stage.at[turn, pl.ds(0, size)], far.at[pl.ds(i * span, size)], left.at[turn]
        )

    def far_group(i, turn):
        def write(low, part):
            stage[turn, pl.ds(low, strip), :] = part

        group(near.shape[0] // span + i, write)

    def far_step(i, carry):
        turn = lax.rem(i, 2)

        @pl.when(i >= 2)
        def _():
            move(i - 2, span, turn).wait()

        far_group(i, turn)
        move(i, span, turn).start()
        return carry

    lax.fori_loop(0, near.shape[0] // span, near_step, 0)
    last = pl.cdiv(far.shape[0], span) - 1
    size = far.shape[0] - last * span
    lax.fori_loop(0, last, far_step, 0)
    move(last - 2, span, last % 2).wait()
    far_group(last, last % 2)
    move(last, size, last % 2).start()
    move(last - 1, span, (last - 1) % 2).wait()
    move(last, size, last % 2).wait()


def count(neighbors, degree, rows):
    slots, nodes = neighbors.shape
    near = PACK * 128 * 4
    arrays = (neighbors, degree)
    return pl.pallas_call(
        count_kernel,
        out_shape=(jax.ShapeDtypeStruct((near, nodes), F8), pltpu.HBM((rows - near, nodes), F8)),
        in_specs=[ANY] * 2,
        out_specs=(VMEM, ANY),
        scratch_shapes=scratch_of(arrays)
        + [
            pltpu.VMEM((slots, nodes), jnp.int32),
            pltpu.VMEM((2, slots, nodes), jnp.int32),
            pltpu.VMEM((2, PACK * 128, nodes), F8),
            pltpu.SemaphoreType.DMA((2,)),
        ],
        compiler_params=LIMIT,
        cost_estimate=cost(9 * 10**9, 20 << 20),
    )(*in_hbm(arrays))


def combine_kernel(table, rows, degree, first, counts_hbm, kept, near, far, out, second, arrived):
    width, nodes = table.shape
    depth = rows.shape[0]
    chunk = 512
    copies = []
    for i in range(second.shape[0] // chunk):
        at = pl.ds(i * chunk, chunk)
        copies.append(pltpu.make_async_copy(counts_hbm.at[at], second.at[at], arrived.at[i]))
        copies[i].start()
    total = jnp.zeros((width, nodes), F32)
    for start in range(0, nodes + 2 * depth, chunk):
        if start < nodes:
            left = table[:, start : start + chunk]
        else:
            h, low = divmod(start - nodes, depth)
            left = rows[low : low + chunk, h * width : (h + 1) * width].astype(F32).T.astype(BF16)
        if start < first.shape[0]:
            counts = first[pl.ds(start, chunk), :]
        else:
            at = start - first.shape[0]
            copies[at // chunk].wait()
            counts = second[pl.ds(at, chunk), :]
        total = total + dot(left, counts.astype(BF16), ((1,), (0,)))
    own = kept[0] + near[0].astype(F32) + far[...].astype(F32)
    result = own + total / degree[...].astype(F32)
    out[...] = jnp.maximum(result, 0.0).astype(BF16)


def combine(table, rows, degree, counts, kept, near, far):
    width, nodes = table.shape
    first, second = counts
    return pl.pallas_call(
        combine_kernel,
        out_shape=jax.ShapeDtypeStruct((width, nodes), BF16),
        in_specs=[VMEM] * 4 + [ANY] + [VMEM] * 3,
        out_specs=VMEM,
        scratch_shapes=[pltpu.VMEM(second.shape, F8), pltpu.SemaphoreType.DMA((second.shape[0] // 512,))],
        compiler_params=LIMIT,
        cost_estimate=cost(2 * width * nodes * 8704, 10 << 20),
    )(table, rows, degree, first, *in_hbm([second]), kept, near, far)


def local(features, proj_in, self_weight, neigh_weight, neighbors, degree, send_rows, send_count):
    columns = lax.axis_size("cols")
    degree = degree[None, :]
    sent = sent_partials(neigh_weight, proj_in, features, columns)
    sent, send_rows = lax.optimization_barrier((sent, send_rows))
    sent = lax.all_to_all(sent, "cols", 0, 0, tiled=True)

    kept, given, wanted = side(self_weight, proj_in, features, send_rows, send_count, columns)
    near = lax.ppermute(given, "cols", [(c, c ^ 1) for c in range(columns)])

    chosen, table = select(sent, wanted)
    chosen, near = lax.optimization_barrier((chosen, near))
    far = (kept[1] + near[1].astype(F32)).astype(BF16)
    chosen, neighbors, far = lax.optimization_barrier((chosen, neighbors, far))
    rows = lax.all_to_all(chosen.reshape(-1, HALF, chosen.shape[1]), "dom", 0, 0, tiled=True)
    far = lax.ppermute(far, "cols", [(c, c ^ 2) for c in range(columns)])
    counts = count(neighbors, degree, neighbors.shape[1] + 2 * chosen.shape[0])
    return combine(table, rows.reshape(chosen.shape), degree, counts, kept, near, far)


def solution(mesh):
    return jax.shard_map(
        local,
        mesh=mesh,
        in_specs=(
            P("cols", "dom"),
            P("cols", None),
            P(),
            P(),
            P(None, "dom"),
            P("dom"),
            P("dom", None),
            P("dom", None),
        ),
        out_specs=P("cols", "dom"),
        check_vma=False,
    )
```

```python
import jax
import jax.numpy as jnp
from jax import lax
from jax.experimental import pallas as pl
from jax.experimental.pallas import tpu as pltpu
from jax.sharding import PartitionSpec as P

F32 = jnp.float32
BF16 = jnp.bfloat16
F8 = jnp.float8_e4m3fn
VMEM = pl.BlockSpec(memory_space=pltpu.VMEM)
ANY = pl.BlockSpec(memory_space=pl.ANY)
LIMIT = pltpu.CompilerParams(vmem_limit_bytes=24 * 1024 * 1024)
CAP = 64
PACK, BITS = 6, 5
HALF = CAP // 2


def cost(flops, nbytes):
    return pl.CostEstimate(flops=flops, bytes_accessed=nbytes, transcendentals=0)


def dot(left, right, dims):
    return lax.dot_general(left, right, (dims, ((), ())), preferred_element_type=F32)


def fetch(sources, targets, arrived):
    copies = [pltpu.make_async_copy(*pair, arrived.at[i]) for i, pair in enumerate(zip(sources, targets))]
    for copy in copies:
        copy.start()
    return copies


def product(copies, weight, proj, features):
    copies[0].wait()
    copies[1].wait()
    joined = dot(weight[...], proj[...], ((0,), (1,)))
    high = joined.astype(BF16)
    low = (joined - high.astype(F32)).astype(BF16)
    copies[2].wait()
    return dot(high, features[...], ((1,), (0,))) + dot(low, features[...], ((1,), (0,)))


def scratch_of(arrays):
    return [pltpu.VMEM(array.shape, array.dtype) for array in arrays] + [pltpu.SemaphoreType.DMA((len(arrays),))]


def in_hbm(arrays):
    return [pltpu.with_memory_space_constraint(array, pltpu.HBM) for array in arrays]


def sent_kernel(weight_hbm, proj_hbm, features_hbm, out, weight, proj, features, arrived):
    copies = fetch((weight_hbm, proj_hbm, features_hbm), (weight, proj, features), arrived)
    out[...] = product(copies, weight, proj, features).astype(BF16).reshape(out.shape)


def sent_partials(weight, proj, features, columns):
    width, nodes = weight.shape[1], features.shape[1]
    arrays = (weight, proj, features)
    return pl.pallas_call(
        sent_kernel,
        out_shape=jax.ShapeDtypeStruct((columns, width // columns, nodes), BF16),
        in_specs=[ANY] * 3,
        out_specs=VMEM,
        scratch_shapes=scratch_of(arrays),
        compiler_params=LIMIT,
        cost_estimate=cost(2 * width * nodes * 640, 1 << 20),
    )(*in_hbm(arrays))


def side_kernel(*refs):
    sources, (kept, given, wanted), targets = refs[:5], refs[5:8], refs[8:13]
    arrived, wide, spread, limits = refs[13:]
    weight, proj, features, rows, live = targets
    copies = fetch(sources, targets, arrived)
    wide[...] = product(copies, weight, proj, features)
    depth = kept.shape[1]
    me = lax.axis_index("cols")
    pair, odd = me // 2, lax.rem(me, 2)
    for i in range(2):
        first = 2 * (pair if i == 0 else 1 - pair)
        start = pl.multiple_of((first + odd) * depth, depth)
        kept[i] = wide[pl.ds(start, depth), :]
        start = pl.multiple_of((first + 1 - odd) * depth, depth)
        given[i] = wide[pl.ds(start, depth), :].astype(BF16)
    copies[3].wait()
    copies[4].wait()
    lines = spread.shape[0]
    for i in range(lines):
        spread[pl.ds(i, 1), :] = rows[:, pl.ds(i * 128, 128)]
    limits[...] = jnp.broadcast_to(live[...], limits.shape).astype(F32).T
    lane = lax.broadcasted_iota(jnp.int32, (lines // 2, 128), 1)
    halves = []
    for k in range(2):
        low = limits[pl.ds(2 * k, lines // 2, stride=4), :]
        high = limits[pl.ds(2 * k + 1, lines // 2, stride=4), :]
        alive = (lane & (CAP - 1)).astype(F32) < jnp.where(lane < CAP, low, high)
        halves.append(jnp.where(alive, spread[pl.ds(k, lines // 2, stride=2), :], -1))
    even, odd = halves
    for h in range(2):
        parts = [pltpu.roll(source, (128 + to - HALF * h) % 128, 1) for source, to in ((even, 0), (even, -32), (odd, 64), (odd, 32))]
        wanted[h] = jnp.where(
            lane < 64, jnp.where(lane < 32, parts[0], parts[1]), jnp.where(lane < 96, parts[2], parts[3])
        )


def side(weight, proj, features, send_rows, send_count, columns):
    width, nodes = weight.shape[1], features.shape[1]
    depth = width // columns
    lines = send_rows.shape[1] // 128
    arrays = (weight, proj, features, send_rows, send_count)
    return pl.pallas_call(
        side_kernel,
        out_shape=(
            jax.ShapeDtypeStruct((2, depth, nodes), F32),
            jax.ShapeDtypeStruct((2, depth, nodes), BF16),
            jax.ShapeDtypeStruct((2, lines // 2, 128), jnp.int32),
        ),
        in_specs=[ANY] * 5,
        out_specs=(VMEM,) * 3,
        scratch_shapes=scratch_of(arrays)
        + [
            pltpu.VMEM((width, nodes), F32),
            pltpu.VMEM((lines, 128), jnp.int32),
            pltpu.VMEM((send_count.shape[1], 128), F32),
        ],
        compiler_params=LIMIT,
        cost_estimate=cost(2 * width * nodes * 640, 1 << 20),
    )(*in_hbm(arrays))


def select_kernel(sent, wanted, rows_hbm, table, rows, left):
    width, nodes = table.shape
    total = sent[0].astype(F32)
    for c in range(1, sent.shape[0]):
        total = total + sent[c].astype(F32)
    table[...] = total.astype(BF16)
    stacked = jnp.concatenate([table[:, :256], table[:, 256:]], axis=0)
    step = 256
    iota = lax.broadcasted_iota(jnp.int32, (256, step), 0).astype(F32).astype(BF16)
    copies = []
    for start in range(0, rows.shape[0], step):
        halves = []
        for h in range(2):
            lines = [wanted[h, pl.ds((start + at) // 128, 1), :] for at in range(0, step, 128)]
            codes = jnp.concatenate(lines, axis=1)
            low = jnp.where(codes >= 0, codes & 255, -1).astype(F32)
            low = jnp.broadcast_to(low, (16, step)).astype(BF16)
            low = jnp.broadcast_to(low[None], (16, 16, step)).reshape(256, step)
            onehot = jnp.where(iota == low, jnp.ones((), BF16), jnp.zeros((), BF16))
            both = dot(stacked, onehot, ((1,), (0,)))
            picked = jnp.where(codes >= 256, both[width:], both[:width])
            halves.append(picked)
        at = pl.ds(start, step)
        rows[at, :] = jnp.concatenate(halves, axis=0).T.astype(BF16)
        copies.append(pltpu.make_async_copy(rows.at[at], rows_hbm.at[at], left.at[len(copies)]))
        copies[-1].start()
    for copy in copies:
        copy.wait()


def select(sent, wanted):
    width, nodes = sent.shape[1], sent.shape[2]
    columns = wanted.shape[1] * 128
    return pl.pallas_call(
        select_kernel,
        out_shape=(
            pltpu.HBM((columns, 2 * width), BF16),
            jax.ShapeDtypeStruct((width, nodes), BF16),
        ),
        in_specs=[VMEM] * 2,
        out_specs=(ANY, VMEM),
        scratch_shapes=[pltpu.VMEM((columns, 2 * width), BF16), pltpu.SemaphoreType.DMA((columns // 256,))],
        compiler_params=LIMIT,
        cost_estimate=cost(4 * width * nodes * columns, 1 << 20),
    )(sent, wanted)


def count_kernel(neighbors_hbm, degree_hbm, near, far, neighbors, degree, arrived, codes, spread, stage, left):
    slots, nodes = codes.shape
    for copy in fetch((neighbors_hbm, degree_hbm), (neighbors, degree), arrived):
        copy.wait()
    rows = near.shape[0] + far.shape[0]
    code = neighbors[...] - nodes
    part, slot = code >> 6, code & (CAP - 1)
    remote = nodes + (slot >> 5) * ((rows - nodes) // 2) + part * HALF + (slot & (HALF - 1))
    used = lax.broadcasted_iota(jnp.int32, (slots, nodes), 0) < degree[...]
    codes[...] = jnp.where(used, jnp.where(code >= 0, remote, code + nodes), -1)
    block, strip = stage.shape[1] // PACK, 32
    span = PACK * block
    iota = lax.broadcasted_iota(jnp.int32, (strip, nodes), 0)

    def group(i, write):
        code = codes[...] - i * span
        inside = jnp.logical_and(code >= 0, code < span)
        spread[0] = jnp.where(inside, code & (block - 1), -1)
        spread[1] = jnp.where(inside, 1 << ((code >> 7) * BITS), 0)
        for low in range(0, block, strip):
            places = iota + low
            total = jnp.zeros((strip, nodes), jnp.int32)
            for k in range(slots):
                total = total + jnp.where(places == spread[0, k : k + 1, :], spread[1, k : k + 1, :], 0)
            for j in range(PACK):
                part = (total >> (j * BITS)) & (2**BITS - 1)
                write(j * block + low, part.astype(F32).astype(F8))

    def near_step(i, carry):
        def write(low, part):
            near[pl.ds(pl.multiple_of(i * span + low, strip), strip), :] = part

        group(i, write)
        return carry

    def move(i, size, turn):
        return pltpu.make_async_copy(
            stage.at[turn, pl.ds(0, size)], far.at[pl.ds(i * span, size)], left.at[turn]
        )

    def far_group(i, turn):
        def write(low, part):
            stage[turn, pl.ds(low, strip), :] = part

        group(near.shape[0] // span + i, write)

    def far_step(i, carry):
        turn = lax.rem(i, 2)

        @pl.when(i >= 2)
        def _():
            move(i - 2, span, turn).wait()

        far_group(i, turn)
        move(i, span, turn).start()
        return carry

    lax.fori_loop(0, near.shape[0] // span, near_step, 0)
    last = pl.cdiv(far.shape[0], span) - 1
    size = far.shape[0] - last * span
    lax.fori_loop(0, last, far_step, 0)
    move(last - 2, span, last % 2).wait()
    far_group(last, last % 2)
    move(last, size, last % 2).start()
    move(last - 1, span, (last - 1) % 2).wait()
    move(last, size, last % 2).wait()


def count(neighbors, degree, rows):
    slots, nodes = neighbors.shape
    near = PACK * 128 * 4
    arrays = (neighbors, degree)
    return pl.pallas_call(
        count_kernel,
        out_shape=(jax.ShapeDtypeStruct((near, nodes), F8), pltpu.HBM((rows - near, nodes), F8)),
        in_specs=[ANY] * 2,
        out_specs=(VMEM, ANY),
        scratch_shapes=scratch_of(arrays)
        + [
            pltpu.VMEM((slots, nodes), jnp.int32),
            pltpu.VMEM((2, slots, nodes), jnp.int32),
            pltpu.VMEM((2, PACK * 128, nodes), F8),
            pltpu.SemaphoreType.DMA((2,)),
        ],
        compiler_params=LIMIT,
        cost_estimate=cost(9 * 10**9, 20 << 20),
    )(*in_hbm(arrays))


def combine_kernel(table, rows, degree, first, counts_hbm, kept, near, far, out, second, arrived):
    width, nodes = table.shape
    depth = rows.shape[0]
    chunk = 512
    copies = []
    for i in range(second.shape[0] // chunk):
        at = pl.ds(i * chunk, chunk)
        copies.append(pltpu.make_async_copy(counts_hbm.at[at], second.at[at], arrived.at[i]))
        copies[i].start()
    turned = []
    total = jnp.zeros((width, nodes), F32)
    for start in range(0, nodes + 2 * depth, chunk):
        if start < nodes:
            left = table[:, start : start + chunk]
        else:
            h, low = divmod(start - nodes, depth)
            if h == 0:
                turned.append(rows[low : low + chunk, :].astype(F32).T.astype(BF16))
            left = turned[low // chunk][h * width : (h + 1) * width]
        if start < first.shape[0]:
            counts = first[pl.ds(start, chunk), :]
        else:
            at = start - first.shape[0]
            copies[at // chunk].wait()
            counts = second[pl.ds(at, chunk), :]
        total = total + dot(left, counts.astype(BF16), ((1,), (0,)))
    own = kept[0] + near[0].astype(F32) + far[...].astype(F32)
    result = own + total / degree[...].astype(F32)
    out[...] = jnp.maximum(result, 0.0).astype(BF16)


def combine(table, rows, degree, counts, kept, near, far):
    width, nodes = table.shape
    first, second = counts
    return pl.pallas_call(
        combine_kernel,
        out_shape=jax.ShapeDtypeStruct((width, nodes), BF16),
        in_specs=[VMEM] * 4 + [ANY] + [VMEM] * 3,
        out_specs=VMEM,
        scratch_shapes=[pltpu.VMEM(second.shape, F8), pltpu.SemaphoreType.DMA((second.shape[0] // 512,))],
        compiler_params=LIMIT,
        cost_estimate=cost(2 * width * nodes * 8704, 10 << 20),
    )(table, rows, degree, first, *in_hbm([second]), kept, near, far)


def local(features, proj_in, self_weight, neigh_weight, neighbors, degree, send_rows, send_count):
    columns = lax.axis_size("cols")
    degree = degree[None, :]
    sent = sent_partials(neigh_weight, proj_in, features, columns)
    sent, send_rows = lax.optimization_barrier((sent, send_rows))
    sent = lax.all_to_all(sent, "cols", 0, 0, tiled=True)

    kept, given, wanted = side(self_weight, proj_in, features, send_rows, send_count, columns)
    near = lax.ppermute(given, "cols", [(c, c ^ 1) for c in range(columns)])

    chosen, table = select(sent, wanted)
    chosen, near = lax.optimization_barrier((chosen, near))
    far = (kept[1] + near[1].astype(F32)).astype(BF16)
    chosen, neighbors, far = lax.optimization_barrier((chosen, neighbors, far))
    rows = lax.all_to_all(chosen.reshape(-1, HALF, chosen.shape[1]), "dom", 0, 0, tiled=True)
    far = lax.ppermute(far, "cols", [(c, c ^ 2) for c in range(columns)])
    counts = count(neighbors, degree, neighbors.shape[1] + 2 * chosen.shape[0])
    return combine(table, rows.reshape(chosen.shape), degree, counts, kept, near, far)


def solution(mesh):
    return jax.shard_map(
        local,
        mesh=mesh,
        in_specs=(
            P("cols", "dom"),
            P("cols", None),
            P(),
            P(),
            P(None, "dom"),
            P("dom"),
            P("dom", None),
            P("dom", None),
        ),
        out_specs=P("cols", "dom"),
        check_vma=False,
    )
```

```python
import jax
import jax.numpy as jnp
from jax import lax
from jax.experimental import pallas as pl
from jax.experimental.pallas import tpu as pltpu
from jax.sharding import PartitionSpec as P

F32 = jnp.float32
BF16 = jnp.bfloat16
F8 = jnp.float8_e4m3fn
VMEM = pl.BlockSpec(memory_space=pltpu.VMEM)
ANY = pl.BlockSpec(memory_space=pl.ANY)
LIMIT = pltpu.CompilerParams(vmem_limit_bytes=24 * 1024 * 1024)
CAP = 64
PACK, BITS = 6, 5
HALF = CAP // 2


def cost(flops, nbytes):
    return pl.CostEstimate(flops=flops, bytes_accessed=nbytes, transcendentals=0)


def dot(left, right, dims):
    return lax.dot_general(left, right, (dims, ((), ())), preferred_element_type=F32)


def fetch(sources, targets, arrived):
    copies = [pltpu.make_async_copy(*pair, arrived.at[i]) for i, pair in enumerate(zip(sources, targets))]
    for copy in copies:
        copy.start()
    return copies


def product(copies, weight, proj, features):
    copies[0].wait()
    copies[1].wait()
    joined = dot(weight[...], proj[...], ((0,), (1,)))
    high = joined.astype(BF16)
    low = (joined - high.astype(F32)).astype(BF16)
    copies[2].wait()
    return dot(high, features[...], ((1,), (0,))) + dot(low, features[...], ((1,), (0,)))


def scratch_of(arrays):
    return [pltpu.VMEM(array.shape, array.dtype) for array in arrays] + [pltpu.SemaphoreType.DMA((len(arrays),))]


def in_hbm(arrays):
    return [pltpu.with_memory_space_constraint(array, pltpu.HBM) for array in arrays]


def sent_kernel(weight_hbm, proj_hbm, features_hbm, out, weight, proj, features, arrived):
    copies = fetch((weight_hbm, proj_hbm, features_hbm), (weight, proj, features), arrived)
    out[...] = product(copies, weight, proj, features).astype(BF16).reshape(out.shape)


def sent_partials(weight, proj, features, columns):
    width, nodes = weight.shape[1], features.shape[1]
    arrays = (weight, proj, features)
    return pl.pallas_call(
        sent_kernel,
        out_shape=jax.ShapeDtypeStruct((columns, width // columns, nodes), BF16),
        in_specs=[ANY] * 3,
        out_specs=VMEM,
        scratch_shapes=scratch_of(arrays),
        compiler_params=LIMIT,
        cost_estimate=cost(2 * width * nodes * 640, 1 << 20),
    )(*in_hbm(arrays))


def side_kernel(*refs):
    sources, (kept, given, wanted), targets = refs[:5], refs[5:8], refs[8:13]
    arrived, wide, spread, limits = refs[13:]
    weight, proj, features, rows, live = targets
    copies = fetch(sources, targets, arrived)
    wide[...] = product(copies, weight, proj, features)
    depth = kept.shape[1]
    me = lax.axis_index("cols")
    pair, odd = me // 2, lax.rem(me, 2)
    for i in range(2):
        first = 2 * (pair if i == 0 else 1 - pair)
        start = pl.multiple_of((first + odd) * depth, depth)
        kept[i] = wide[pl.ds(start, depth), :]
        start = pl.multiple_of((first + 1 - odd) * depth, depth)
        given[i] = wide[pl.ds(start, depth), :].astype(BF16)
    copies[3].wait()
    copies[4].wait()
    lines = spread.shape[0]
    for i in range(lines):
        spread[pl.ds(i, 1), :] = rows[:, pl.ds(i * 128, 128)]
    limits[...] = jnp.broadcast_to(live[...], limits.shape).astype(F32).T
    lane = lax.broadcasted_iota(jnp.int32, (lines // 2, 128), 1)
    halves = []
    for k in range(2):
        low = limits[pl.ds(2 * k, lines // 2, stride=4), :]
        high = limits[pl.ds(2 * k + 1, lines // 2, stride=4), :]
        alive = (lane & (CAP - 1)).astype(F32) < jnp.where(lane < CAP, low, high)
        halves.append(jnp.where(alive, spread[pl.ds(k, lines // 2, stride=2), :], -1))
    even, odd = halves
    for h in range(2):
        parts = [pltpu.roll(source, (128 + to - HALF * h) % 128, 1) for source, to in ((even, 0), (even, -32), (odd, 64), (odd, 32))]
        wanted[h] = jnp.where(
            lane < 64, jnp.where(lane < 32, parts[0], parts[1]), jnp.where(lane < 96, parts[2], parts[3])
        )


def side(weight, proj, features, send_rows, send_count, columns):
    width, nodes = weight.shape[1], features.shape[1]
    depth = width // columns
    lines = send_rows.shape[1] // 128
    arrays = (weight, proj, features, send_rows, send_count)
    return pl.pallas_call(
        side_kernel,
        out_shape=(
            jax.ShapeDtypeStruct((2, depth, nodes), F32),
            jax.ShapeDtypeStruct((2, depth, nodes), BF16),
            jax.ShapeDtypeStruct((2, lines // 2, 128), jnp.int32),
        ),
        in_specs=[ANY] * 5,
        out_specs=(VMEM,) * 3,
        scratch_shapes=scratch_of(arrays)
        + [
            pltpu.VMEM((width, nodes), F32),
            pltpu.VMEM((lines, 128), jnp.int32),
            pltpu.VMEM((send_count.shape[1], 128), F32),
        ],
        compiler_params=LIMIT,
        cost_estimate=cost(2 * width * nodes * 640, 1 << 20),
    )(*in_hbm(arrays))


def select_kernel(sent, wanted, rows_hbm, table, rows, left):
    width, nodes = table.shape
    total = sent[0].astype(F32)
    for c in range(1, sent.shape[0]):
        total = total + sent[c].astype(F32)
    table[...] = total.astype(BF16)
    stacked = jnp.concatenate([table[:, :256], table[:, 256:]], axis=0)
    step = 256
    iota = lax.broadcasted_iota(jnp.int32, (256, step), 0).astype(F32).astype(BF16)
    copies = []
    for start in range(0, rows.shape[0], step):
        halves = []
        for h in range(2):
            lines = [wanted[h, pl.ds((start + at) // 128, 1), :] for at in range(0, step, 128)]
            codes = jnp.concatenate(lines, axis=1)
            low = jnp.where(codes >= 0, codes & 255, -1).astype(F32)
            low = jnp.broadcast_to(low, (16, step)).astype(BF16)
            low = jnp.broadcast_to(low[None], (16, 16, step)).reshape(256, step)
            onehot = jnp.where(iota == low, jnp.ones((), BF16), jnp.zeros((), BF16))
            both = dot(stacked, onehot, ((1,), (0,)))
            picked = jnp.where(codes >= 256, both[width:], both[:width])
            halves.append(picked)
        at = pl.ds(start, step)
        rows[at, :] = jnp.concatenate(halves, axis=0).T.astype(BF16)
        copies.append(pltpu.make_async_copy(rows.at[at], rows_hbm.at[at], left.at[len(copies)]))
        copies[-1].start()
    for copy in copies:
        copy.wait()


def select(sent, wanted):
    width, nodes = sent.shape[1], sent.shape[2]
    columns = wanted.shape[1] * 128
    return pl.pallas_call(
        select_kernel,
        out_shape=(
            pltpu.HBM((columns, 2 * width), BF16),
            jax.ShapeDtypeStruct((width, nodes), BF16),
        ),
        in_specs=[VMEM] * 2,
        out_specs=(ANY, VMEM),
        scratch_shapes=[pltpu.VMEM((columns, 2 * width), BF16), pltpu.SemaphoreType.DMA((columns // 256,))],
        compiler_params=LIMIT,
        cost_estimate=cost(4 * width * nodes * columns, 1 << 20),
    )(sent, wanted)


def count_kernel(neighbors_hbm, degree_hbm, near, far, neighbors, degree, arrived, codes, spread, stage, left):
    slots, nodes = codes.shape
    for copy in fetch((neighbors_hbm, degree_hbm), (neighbors, degree), arrived):
        copy.wait()
    rows = near.shape[0] + far.shape[0]
    code = neighbors[...] - nodes
    part, slot = code >> 6, code & (CAP - 1)
    remote = nodes + (slot >> 5) * ((rows - nodes) // 2) + part * HALF + (slot & (HALF - 1))
    used = lax.broadcasted_iota(jnp.int32, (slots, nodes), 0) < degree[...]
    codes[...] = jnp.where(used, jnp.where(code >= 0, remote, code + nodes), -1)
    block, strip = stage.shape[1] // PACK, 32
    span = PACK * block
    iota = lax.broadcasted_iota(jnp.int32, (strip, nodes), 0)

    def group(i, write):
        code = codes[...] - i * span
        inside = jnp.logical_and(code >= 0, code < span)
        spread[0] = jnp.where(inside, code & (block - 1), -1)
        spread[1] = jnp.where(inside, 1 << ((code >> 7) * BITS), 0)
        for low in range(0, block, strip):
            places = iota + low
            total = jnp.zeros((strip, nodes), jnp.int32)
            for k in range(slots):
                total = total + jnp.where(places == spread[0, k : k + 1, :], spread[1, k : k + 1, :], 0)
            for j in range(PACK):
                part = (total >> (j * BITS)) & (2**BITS - 1)
                write(j * block + low, part.astype(F32).astype(F8))

    def near_step(i, carry):
        def write(low, part):
            near[pl.ds(pl.multiple_of(i * span + low, strip), strip), :] = part

        group(i, write)
        return carry

    def move(i, size, turn):
        return pltpu.make_async_copy(
            stage.at[turn, pl.ds(0, size)], far.at[pl.ds(i * span, size)], left.at[turn]
        )

    def far_group(i, turn):
        def write(low, part):
            stage[turn, pl.ds(low, strip), :] = part

        group(near.shape[0] // span + i, write)

    def far_step(i, carry):
        turn = lax.rem(i, 2)

        @pl.when(i >= 2)
        def _():
            move(i - 2, span, turn).wait()

        far_group(i, turn)
        move(i, span, turn).start()
        return carry

    lax.fori_loop(0, near.shape[0] // span, near_step, 0)
    last = pl.cdiv(far.shape[0], span) - 1
    size = far.shape[0] - last * span
    lax.fori_loop(0, last, far_step, 0)
    move(last - 2, span, last % 2).wait()
    far_group(last, last % 2)
    move(last, size, last % 2).start()
    move(last - 1, span, (last - 1) % 2).wait()
    move(last, size, last % 2).wait()


def count(neighbors, degree, rows):
    slots, nodes = neighbors.shape
    near = PACK * 128 * 4
    arrays = (neighbors, degree)
    return pl.pallas_call(
        count_kernel,
        out_shape=(jax.ShapeDtypeStruct((near, nodes), F8), pltpu.HBM((rows - near, nodes), F8)),
        in_specs=[ANY] * 2,
        out_specs=(VMEM, ANY),
        scratch_shapes=scratch_of(arrays)
        + [
            pltpu.VMEM((slots, nodes), jnp.int32),
            pltpu.VMEM((2, slots, nodes), jnp.int32),
            pltpu.VMEM((2, PACK * 128, nodes), F8),
            pltpu.SemaphoreType.DMA((2,)),
        ],
        compiler_params=LIMIT,
        cost_estimate=cost(9 * 10**9, 20 << 20),
    )(*in_hbm(arrays))


def combine_kernel(table, rows, degree, first, counts_hbm, kept, near, far, out, second, arrived):
    width, nodes = table.shape
    depth = rows.shape[0]
    chunk = 512
    copies = []
    for i in range(second.shape[0] // chunk):
        at = pl.ds(i * chunk, chunk)
        copies.append(pltpu.make_async_copy(counts_hbm.at[at], second.at[at], arrived.at[i]))
        copies[i].start()
    turned = []
    total = jnp.zeros((width, nodes), F32)
    for start in range(0, nodes + 2 * depth, chunk):
        if start < nodes:
            left = table[:, start : start + chunk]
        else:
            h, low = divmod(start - nodes, depth)
            if h == 0:
                turned.append(rows[low : low + chunk, :].astype(F32).T.astype(BF16))
            left = turned[low // chunk][h * width : (h + 1) * width]
        if start < first.shape[0]:
            counts = first[pl.ds(start, chunk), :]
        else:
            at = start - first.shape[0]
            copies[at // chunk].wait()
            counts = second[pl.ds(at, chunk), :]
        total = total + dot(left, counts, ((1,), (0,)))
    own = kept[0] + near[0].astype(F32) + far[...].astype(F32)
    result = own + total / degree[...].astype(F32)
    out[...] = jnp.maximum(result, 0.0).astype(BF16)


def combine(table, rows, degree, counts, kept, near, far):
    width, nodes = table.shape
    first, second = counts
    return pl.pallas_call(
        combine_kernel,
        out_shape=jax.ShapeDtypeStruct((width, nodes), BF16),
        in_specs=[VMEM] * 4 + [ANY] + [VMEM] * 3,
        out_specs=VMEM,
        scratch_shapes=[pltpu.VMEM(second.shape, F8), pltpu.SemaphoreType.DMA((second.shape[0] // 512,))],
        compiler_params=LIMIT,
        cost_estimate=cost(2 * width * nodes * 8704, 10 << 20),
    )(table, rows, degree, first, *in_hbm([second]), kept, near, far)


def local(features, proj_in, self_weight, neigh_weight, neighbors, degree, send_rows, send_count):
    columns = lax.axis_size("cols")
    degree = degree[None, :]
    sent = sent_partials(neigh_weight, proj_in, features, columns)
    sent, send_rows = lax.optimization_barrier((sent, send_rows))
    sent = lax.all_to_all(sent, "cols", 0, 0, tiled=True)

    kept, given, wanted = side(self_weight, proj_in, features, send_rows, send_count, columns)
    near = lax.ppermute(given, "cols", [(c, c ^ 1) for c in range(columns)])

    chosen, table = select(sent, wanted)
    chosen, near = lax.optimization_barrier((chosen, near))
    far = (kept[1] + near[1].astype(F32)).astype(BF16)
    chosen, neighbors, far = lax.optimization_barrier((chosen, neighbors, far))
    rows = lax.all_to_all(chosen.reshape(-1, HALF, chosen.shape[1]), "dom", 0, 0, tiled=True)
    far = lax.ppermute(far, "cols", [(c, c ^ 2) for c in range(columns)])
    counts = count(neighbors, degree, neighbors.shape[1] + 2 * chosen.shape[0])
    return combine(table, rows.reshape(chosen.shape), degree, counts, kept, near, far)


def solution(mesh):
    return jax.shard_map(
        local,
        mesh=mesh,
        in_specs=(
            P("cols", "dom"),
            P("cols", None),
            P(),
            P(),
            P(None, "dom"),
            P("dom"),
            P("dom", None),
            P("dom", None),
        ),
        out_specs=P("cols", "dom"),
        check_vma=False,
    )
```

```python
import jax
import jax.numpy as jnp
from jax import lax
from jax.experimental import pallas as pl
from jax.experimental.pallas import tpu as pltpu
from jax.sharding import PartitionSpec as P

F32 = jnp.float32
BF16 = jnp.bfloat16
F8 = jnp.float8_e4m3fn
VMEM = pl.BlockSpec(memory_space=pltpu.VMEM)
ANY = pl.BlockSpec(memory_space=pl.ANY)
LIMIT = pltpu.CompilerParams(vmem_limit_bytes=24 * 1024 * 1024)
CAP = 64
PACK, BITS = 6, 5
HALF = CAP // 2


def cost(flops, nbytes):
    return pl.CostEstimate(flops=flops, bytes_accessed=nbytes, transcendentals=0)


def dot(left, right, dims):
    return lax.dot_general(left, right, (dims, ((), ())), preferred_element_type=F32)


def fetch(sources, targets, arrived):
    copies = [pltpu.make_async_copy(*pair, arrived.at[i]) for i, pair in enumerate(zip(sources, targets))]
    for copy in copies:
        copy.start()
    return copies


def product(copies, weight, proj, features):
    copies[0].wait()
    copies[1].wait()
    joined = dot(weight[...], proj[...], ((0,), (1,)))
    high = joined.astype(BF16)
    low = (joined - high.astype(F32)).astype(BF16)
    copies[2].wait()
    return dot(high, features[...], ((1,), (0,))) + dot(low, features[...], ((1,), (0,)))


def scratch_of(arrays):
    return [pltpu.VMEM(array.shape, array.dtype) for array in arrays] + [pltpu.SemaphoreType.DMA((len(arrays),))]


def in_hbm(arrays):
    return [pltpu.with_memory_space_constraint(array, pltpu.HBM) for array in arrays]


def sent_kernel(weight_hbm, proj_hbm, features_hbm, out, weight, proj, features, arrived):
    copies = fetch((weight_hbm, proj_hbm, features_hbm), (weight, proj, features), arrived)
    out[...] = product(copies, weight, proj, features).astype(BF16).reshape(out.shape)


def sent_partials(weight, proj, features, columns):
    width, nodes = weight.shape[1], features.shape[1]
    arrays = (weight, proj, features)
    return pl.pallas_call(
        sent_kernel,
        out_shape=jax.ShapeDtypeStruct((columns, width // columns, nodes), BF16),
        in_specs=[ANY] * 3,
        out_specs=VMEM,
        scratch_shapes=scratch_of(arrays),
        compiler_params=LIMIT,
        cost_estimate=cost(2 * width * nodes * 640, 1 << 20),
    )(*in_hbm(arrays))


def side_kernel(*refs):
    sources, (kept, given, wanted), targets = refs[:5], refs[5:8], refs[8:13]
    arrived, wide, spread, limits = refs[13:]
    weight, proj, features, rows, live = targets
    copies = fetch(sources, targets, arrived)
    wide[...] = product(copies, weight, proj, features)
    depth = kept.shape[1]
    me = lax.axis_index("cols")
    pair, odd = me // 2, lax.rem(me, 2)
    for i in range(2):
        first = 2 * (pair if i == 0 else 1 - pair)
        start = pl.multiple_of((first + odd) * depth, depth)
        kept[i] = wide[pl.ds(start, depth), :]
        start = pl.multiple_of((first + 1 - odd) * depth, depth)
        given[i] = wide[pl.ds(start, depth), :].astype(BF16)
    copies[3].wait()
    copies[4].wait()
    lines = spread.shape[0]
    for i in range(lines):
        spread[pl.ds(i, 1), :] = rows[:, pl.ds(i * 128, 128)]
    limits[...] = jnp.broadcast_to(live[...], limits.shape).astype(F32).T
    lane = lax.broadcasted_iota(jnp.int32, (lines // 2, 128), 1)
    halves = []
    for k in range(2):
        low = limits[pl.ds(2 * k, lines // 2, stride=4), :]
        high = limits[pl.ds(2 * k + 1, lines // 2, stride=4), :]
        alive = (lane & (CAP - 1)).astype(F32) < jnp.where(lane < CAP, low, high)
        halves.append(jnp.where(alive, spread[pl.ds(k, lines // 2, stride=2), :], -1))
    even, odd = halves
    for h in range(2):
        parts = [pltpu.roll(source, (128 + to - HALF * h) % 128, 1) for source, to in ((even, 0), (even, -32), (odd, 64), (odd, 32))]
        wanted[h] = jnp.where(
            lane < 64, jnp.where(lane < 32, parts[0], parts[1]), jnp.where(lane < 96, parts[2], parts[3])
        )


def side(weight, proj, features, send_rows, send_count, columns):
    width, nodes = weight.shape[1], features.shape[1]
    depth = width // columns
    lines = send_rows.shape[1] // 128
    arrays = (weight, proj, features, send_rows, send_count)
    return pl.pallas_call(
        side_kernel,
        out_shape=(
            jax.ShapeDtypeStruct((2, depth, nodes), F32),
            jax.ShapeDtypeStruct((2, depth, nodes), BF16),
            jax.ShapeDtypeStruct((2, lines // 2, 128), jnp.int32),
        ),
        in_specs=[ANY] * 5,
        out_specs=(VMEM,) * 3,
        scratch_shapes=scratch_of(arrays)
        + [
            pltpu.VMEM((width, nodes), F32),
            pltpu.VMEM((lines, 128), jnp.int32),
            pltpu.VMEM((send_count.shape[1], 128), F32),
        ],
        compiler_params=LIMIT,
        cost_estimate=cost(2 * width * nodes * 640, 1 << 20),
    )(*in_hbm(arrays))


def select_kernel(sent, wanted, rows_hbm, table, rows, left):
    width, nodes = table.shape
    total = sent[0].astype(F32)
    for c in range(1, sent.shape[0]):
        total = total + sent[c].astype(F32)
    table[...] = total.astype(BF16)
    stacked = jnp.concatenate([table[:, :256], table[:, 256:]], axis=0)
    step = 256
    iota = lax.broadcasted_iota(jnp.int32, (256, step), 0).astype(F32).astype(BF16)
    copies = []
    for start in range(0, rows.shape[0], step):
        halves = []
        for h in range(2):
            lines = [wanted[h, pl.ds((start + at) // 128, 1), :] for at in range(0, step, 128)]
            codes = jnp.concatenate(lines, axis=1)
            low = jnp.where(codes >= 0, codes & 255, -1).astype(F32)
            low = jnp.broadcast_to(low, (16, step)).astype(BF16)
            low = jnp.broadcast_to(low[None], (16, 16, step)).reshape(256, step)
            onehot = jnp.where(iota == low, jnp.ones((), BF16), jnp.zeros((), BF16))
            both = dot(stacked, onehot, ((1,), (0,)))
            picked = jnp.where(codes >= 256, both[width:], both[:width])
            halves.append(picked)
        at = pl.ds(start, step)
        rows[at, :] = jnp.concatenate(halves, axis=0).T.astype(BF16)
        copies.append(pltpu.make_async_copy(rows.at[at], rows_hbm.at[at], left.at[len(copies)]))
        copies[-1].start()
    for copy in copies:
        copy.wait()


def select(sent, wanted):
    width, nodes = sent.shape[1], sent.shape[2]
    columns = wanted.shape[1] * 128
    return pl.pallas_call(
        select_kernel,
        out_shape=(
            pltpu.HBM((columns, 2 * width), BF16),
            jax.ShapeDtypeStruct((width, nodes), BF16),
        ),
        in_specs=[VMEM] * 2,
        out_specs=(ANY, VMEM),
        scratch_shapes=[pltpu.VMEM((columns, 2 * width), BF16), pltpu.SemaphoreType.DMA((columns // 256,))],
        compiler_params=LIMIT,
        cost_estimate=cost(4 * width * nodes * columns, 1 << 20),
    )(sent, wanted)


def count_kernel(neighbors_hbm, degree_hbm, near, far, neighbors, degree, arrived, codes, spread, stage, left):
    slots, nodes = codes.shape
    for copy in fetch((neighbors_hbm, degree_hbm), (neighbors, degree), arrived):
        copy.wait()
    rows = near.shape[0] + far.shape[0]
    code = neighbors[...] - nodes
    part, slot = code >> 6, code & (CAP - 1)
    remote = nodes + (slot >> 5) * ((rows - nodes) // 2) + part * HALF + (slot & (HALF - 1))
    used = lax.broadcasted_iota(jnp.int32, (slots, nodes), 0) < degree[...]
    codes[...] = jnp.where(used, jnp.where(code >= 0, remote, code + nodes), -1)
    block, strip = stage.shape[1] // PACK, 32
    span = PACK * block
    iota = lax.broadcasted_iota(jnp.int32, (strip, nodes), 0)

    def group(i, write):
        code = codes[...] - i * span
        inside = jnp.logical_and(code >= 0, code < span)
        spread[0] = jnp.where(inside, code & (block - 1), -1)
        spread[1] = jnp.where(inside, 1 << ((code >> 7) * BITS), 0)
        for low in range(0, block, strip):
            places = iota + low
            total = jnp.zeros((strip, nodes), jnp.int32)
            for k in range(slots):
                total = total + jnp.where(places == spread[0, k : k + 1, :], spread[1, k : k + 1, :], 0)
            for j in range(PACK):
                part = (total >> (j * BITS)) & (2**BITS - 1)
                write(j * block + low, part.astype(F32).astype(F8))

    def near_step(i, carry):
        def write(low, part):
            near[pl.ds(pl.multiple_of(i * span + low, strip), strip), :] = part

        group(i, write)
        return carry

    def move(i, size, turn):
        return pltpu.make_async_copy(
            stage.at[turn, pl.ds(0, size)], far.at[pl.ds(i * span, size)], left.at[turn]
        )

    def far_group(i, turn):
        def write(low, part):
            stage[turn, pl.ds(low, strip), :] = part

        group(near.shape[0] // span + i, write)

    def far_step(i, carry):
        turn = lax.rem(i, 2)

        @pl.when(i >= 2)
        def _():
            move(i - 2, span, turn).wait()

        far_group(i, turn)
        move(i, span, turn).start()
        return carry

    lax.fori_loop(0, near.shape[0] // span, near_step, 0)
    last = pl.cdiv(far.shape[0], span) - 1
    size = far.shape[0] - last * span
    lax.fori_loop(0, last, far_step, 0)
    move(last - 2, span, last % 2).wait()
    far_group(last, last % 2)
    move(last, size, last % 2).start()
    move(last - 1, span, (last - 1) % 2).wait()
    move(last, size, last % 2).wait()


def count(neighbors, degree, rows):
    slots, nodes = neighbors.shape
    near = PACK * 128 * 5
    arrays = (neighbors, degree)
    return pl.pallas_call(
        count_kernel,
        out_shape=(jax.ShapeDtypeStruct((near, nodes), F8), pltpu.HBM((rows - near, nodes), F8)),
        in_specs=[ANY] * 2,
        out_specs=(VMEM, ANY),
        scratch_shapes=scratch_of(arrays)
        + [
            pltpu.VMEM((slots, nodes), jnp.int32),
            pltpu.VMEM((2, slots, nodes), jnp.int32),
            pltpu.VMEM((2, PACK * 128, nodes), F8),
            pltpu.SemaphoreType.DMA((2,)),
        ],
        compiler_params=LIMIT,
        cost_estimate=cost(9 * 10**9, 20 << 20),
    )(*in_hbm(arrays))


def combine_kernel(table, rows, degree, first, counts_hbm, kept, near, far, out, second, arrived):
    width, nodes = table.shape
    depth = rows.shape[0]
    chunk = 512
    pieces = []
    for start in range(0, nodes + 2 * depth, chunk):
        middle = min(max(first.shape[0], start), start + chunk)
        pieces += [(low, high - low) for low, high in ((start, middle), (middle, start + chunk)) if high > low]
    copies = {}
    for start, size in pieces:
        if start >= first.shape[0]:
            at = pl.ds(start - first.shape[0], size)
            copies[start] = pltpu.make_async_copy(counts_hbm.at[at], second.at[at], arrived.at[len(copies)])
            copies[start].start()
    turned = []
    total = jnp.zeros((width, nodes), F32)
    for start, size in pieces:
        if start < nodes:
            left = table[:, start : start + size]
        else:
            h, low = divmod(start - nodes, depth)
            if h == 0 and low % chunk == 0:
                turned.append(rows[low : low + chunk, :].astype(F32).T.astype(BF16))
            left = turned[low // chunk][h * width : (h + 1) * width, low % chunk : low % chunk + size]
        if start < first.shape[0]:
            counts = first[pl.ds(start, size), :]
        else:
            copies[start].wait()
            counts = second[pl.ds(start - first.shape[0], size), :]
        total = total + dot(left, counts, ((1,), (0,)))
    own = kept[0] + near[0].astype(F32) + far[...].astype(F32)
    result = own + total / degree[...].astype(F32)
    out[...] = jnp.maximum(result, 0.0).astype(BF16)


def combine(table, rows, degree, counts, kept, near, far):
    width, nodes = table.shape
    first, second = counts
    return pl.pallas_call(
        combine_kernel,
        out_shape=jax.ShapeDtypeStruct((width, nodes), BF16),
        in_specs=[VMEM] * 4 + [ANY] + [VMEM] * 3,
        out_specs=VMEM,
        scratch_shapes=[pltpu.VMEM(second.shape, F8), pltpu.SemaphoreType.DMA((pl.cdiv(second.shape[0], 512),))],
        compiler_params=LIMIT,
        cost_estimate=cost(2 * width * nodes * 8704, 10 << 20),
    )(table, rows, degree, first, *in_hbm([second]), kept, near, far)


def local(features, proj_in, self_weight, neigh_weight, neighbors, degree, send_rows, send_count):
    columns = lax.axis_size("cols")
    degree = degree[None, :]
    sent = sent_partials(neigh_weight, proj_in, features, columns)
    sent, send_rows = lax.optimization_barrier((sent, send_rows))
    sent = lax.all_to_all(sent, "cols", 0, 0, tiled=True)

    kept, given, wanted = side(self_weight, proj_in, features, send_rows, send_count, columns)
    near = lax.ppermute(given, "cols", [(c, c ^ 1) for c in range(columns)])

    chosen, table = select(sent, wanted)
    chosen, near = lax.optimization_barrier((chosen, near))
    far = (kept[1] + near[1].astype(F32)).astype(BF16)
    chosen, neighbors, far = lax.optimization_barrier((chosen, neighbors, far))
    rows = lax.all_to_all(chosen.reshape(-1, HALF, chosen.shape[1]), "dom", 0, 0, tiled=True)
    far = lax.ppermute(far, "cols", [(c, c ^ 2) for c in range(columns)])
    counts = count(neighbors, degree, neighbors.shape[1] + 2 * chosen.shape[0])
    return combine(table, rows.reshape(chosen.shape), degree, counts, kept, near, far)


def solution(mesh):
    return jax.shard_map(
        local,
        mesh=mesh,
        in_specs=(
            P("cols", "dom"),
            P("cols", None),
            P(),
            P(),
            P(None, "dom"),
            P("dom"),
            P("dom", None),
            P("dom", None),
        ),
        out_specs=P("cols", "dom"),
        check_vma=False,
    )
```
